512 devices in a mesh: dp: 64 (over y, z), tensor: 8 (over x, core).
Axes of the slice: x: 4, y: 8, z: 8, core: 2. Of those that a mesh axis runs over, the one named last changes fastest.
Arguments:
- hidden_act: bfloat16 [28672, 28672], P('dp', 'tensor'), may hold values from -160 to 160
- grad_out: bfloat16 [28672, 8192], P('dp', 'tensor'), may hold values from -160 to 160
- proj_in: bfloat16 [28672, 64], P('tensor'), may hold values from -0.03125 to 0.03125
- proj_out: bfloat16 [8192, 64], P('tensor'), may hold values from -0.0625 to 0.0625
- queries: float32 [64, 4096], P('dp'), may hold values from -6 to 6
Outputs:
- example_grads: float32 [256, 4096], P('dp')
- factor_in: float32 [64, 64], replicated
- factor_out: float32 [64, 64], replicated
- scores: float32 [256, 64], P('dp')
The draws below stay inside these ranges and needn't reach their ends.
All inputs are finite; a program needn't handle non-finite values.
Results may differ from the reference program's by a relative error of at most 0.0003.
Values sent between devices are 32-bit elements; how exact they have to be, the bound alone decides.
No kernel may reach another device: no remote copies, remote signals or barrier semaphores. Data moves between devices by JAX's collectives and lax.ppermute only.
A program may use at most 64 MiB of HBM per device.

```python
import math
import jax
import jax.numpy as jnp
from jax import lax

D = 8192
FF = 28672
K = 64
TOK_EX = 112
EXAMPLES = 256
TOKENS = 28672
NQ = 64


def shaped_rows(key, base):
    row_count = base.shape[0]
    key_scale = jax.random.fold_in(key, 1)
    key_dir = jax.random.fold_in(key, 2)
    key_coef = jax.random.fold_in(key, 3)
    position = jnp.arange(row_count, dtype=jnp.float32)[:, None] / float(row_count)
    jitter = jax.random.uniform(key_scale, (row_count, 1), jnp.float32, -0.5, 0.5)
    row_scale = jnp.exp(math.log(3.0) * position + math.log(2.0) * jitter)
    direction = jnp.clip(jax.random.normal(key_dir, (1, base.shape[1]), jnp.float32), -4.0, 4.0)
    weights = jnp.clip(jax.random.normal(key_coef, (row_count, 1), jnp.float32), -4.0, 4.0)
    return row_scale * (base + weights * direction)


def draw_hidden_act(key, part):
    key = jax.random.fold_in(key, 11)
    key_base = jax.random.fold_in(key, 5)
    base = jnp.clip(jax.random.normal(key_base, (TOKENS, FF), jnp.float32), -6.0, 6.0)
    values = shaped_rows(key, base)
    return values.astype(jnp.bfloat16)


def draw_grad_out(key, part):
    key = jax.random.fold_in(key, 23)
    key_base = jax.random.fold_in(key, 5)
    base = jnp.clip(jax.random.normal(key_base, (TOKENS, D), jnp.float32), -6.0, 6.0)
    values = shaped_rows(key, base)
    return values.astype(jnp.bfloat16)


def steps_of(stream_key, dims, cuts, smallest, top_value):
    def one(dim, blocks):
        heights = jax.random.uniform(jax.random.fold_in(jax.random.fold_in(stream_key, 6), dim), (blocks,), jnp.float32, smallest / len(cuts), top_value / len(cuts))
        return jnp.repeat(jnp.exp(heights), dims[dim] // blocks).reshape((-1,) + (1,) * (len(dims) - dim - 1))

    gain = one(*cuts[0])
    for cut in cuts[1:]:
        gain = gain * one(*cut)
    return gain


def gaussian(rng, extent, scale, reach, cuts=(), kind=jnp.bfloat16):
    values = jax.random.normal(rng, extent, jnp.float32) * scale
    if len(cuts) > 0:
        values = steps_of(rng, extent, cuts, -0.22, 0.18) * values
    return jnp.clip(values, min=-reach, max=reach).astype(kind)


def setup_inputs(seed: int = 0) -> dict:
    key_of = jax.random.split(jax.random.key(seed), 6)
    hidden_act = draw_hidden_act(jax.random.fold_in(key_of[5], 71), 0)
    grad_out = draw_grad_out(jax.random.fold_in(key_of[5], 71), 0)
    proj_in = gaussian(key_of[2], (FF, K), FF ** -0.5, 0.03125, ((0, 8),))
    proj_out = gaussian(key_of[3], (D, K), D ** -0.5, 0.0625, ((0, 8),))
    queries = gaussian(key_of[4], (NQ, K * K), 1.0, 6.0, ((0, 64),), jnp.float32)
    return dict(hidden_act=hidden_act, grad_out=grad_out, proj_in=proj_in, proj_out=proj_out, queries=queries)


damping_level = 0.1

def precondition(flat, chol_in, chol_out):
    item_count = flat.shape[0]
    columns = chol_in.shape[0]
    matrices = flat.reshape(item_count, columns, columns)
    stacked = matrices.transpose(1, 0, 2).reshape(columns, item_count * columns)
    solved = jax.scipy.linalg.cho_solve((chol_in, True), stacked)
    solved = solved.reshape(columns, item_count, columns).transpose(2, 1, 0).reshape(columns, item_count * columns)
    solved = jax.scipy.linalg.cho_solve((chol_out, True), solved)
    solved = solved.reshape(columns, item_count, columns).transpose(1, 2, 0)
    return solved.reshape(item_count, columns * columns)

def reference(hidden_act, grad_out, proj_in, proj_out, queries):
    in_proj = jnp.dot(hidden_act.astype(jnp.float32), proj_in.astype(jnp.float32), preferred_element_type=jnp.float32)
    out_proj = jnp.dot(grad_out.astype(jnp.float32), proj_out.astype(jnp.float32), preferred_element_type=jnp.float32)
    eye_mat = jnp.eye(K, dtype=jnp.float32)
    factor_in = jnp.dot(in_proj.T, in_proj, precision=lax.Precision.HIGHEST) / float(TOKENS) + damping_level * eye_mat
    factor_out = jnp.dot(out_proj.T, out_proj, precision=lax.Precision.HIGHEST) / float(TOKENS) + damping_level * eye_mat
    in_ex = in_proj.reshape(EXAMPLES, TOK_EX, K)
    out_ex = out_proj.reshape(EXAMPLES, TOK_EX, K)
    example_grads = jnp.einsum('eti,eto->eio', in_ex, out_ex, precision=lax.Precision.HIGHEST)
    example_grads = (example_grads / math.sqrt(TOK_EX)).reshape(EXAMPLES, K * K)
    chol_in = jnp.linalg.cholesky(factor_in)
    chol_out = jnp.linalg.cholesky(factor_out)
    ready = precondition(queries, chol_in, chol_out)
    scores = jnp.dot(example_grads, ready.T, precision=lax.Precision.HIGHEST) / float(K)
    return (example_grads, factor_in, factor_out, scores)
```

```python
import math

import jax
import jax.numpy as jnp
from jax import lax
from jax.sharding import PartitionSpec as P

EX_DEV = 4
TOK_EX = 112
K = 64
NY = 8
NZ = 8
NT = 8


damping_level = 0.1

Y_GROUPS = [[y * NZ + z for y in range(NY)] for z in range(NZ)]
Z_GROUPS = [[y * NZ + z for z in range(NZ)] for y in range(NY)]


def swap_pairs():
    pairs = []
    for y in range(NY):
        for z in range(NZ):
            for t in range(NT):
                pairs.append(((y * NZ + z) * NT + t, (y * NZ + t) * NT + z))
    return pairs


def spread(x, count):
    return jnp.broadcast_to(x[None], (count,) + x.shape)


def local(hidden_act, grad_out, proj_in, proj_out, queries):
    row_count = hidden_act.shape[0]
    all_tokens = float(row_count * lax.axis_size("dp"))
    my_query = lax.ppermute(queries.reshape(32, 128), ("dp", "tensor"), swap_pairs())
    in_part = jnp.dot(hidden_act, proj_in, preferred_element_type=jnp.float32)
    out_part = jnp.dot(grad_out, proj_out, preferred_element_type=jnp.float32)
    part = jnp.concatenate([in_part, out_part], axis=1).reshape(NT, row_count // NT, 2 * K)
    mine = lax.all_to_all(part, "tensor", 0, 0).sum(0)
    summed = lax.all_to_all(spread(mine, NT), "tensor", 0, 0).reshape(row_count, 2 * K)
    in_proj = summed[:, :K]
    out_proj = summed[:, K:]
    sum_in = jnp.dot(in_proj.T, in_proj, precision=lax.Precision.HIGHEST)
    sum_out = jnp.dot(out_proj.T, out_proj, precision=lax.Precision.HIGHEST)
    rows = lax.broadcasted_iota(jnp.int32, (K, K), 0)
    cols = lax.broadcasted_iota(jnp.int32, (K, K), 1)
    eye_mat = jnp.eye(K, dtype=jnp.float32)
    square = jnp.where(rows >= cols, sum_in, sum_out)
    diag = jnp.sum(sum_out * eye_mat, axis=0)
    packed = jnp.concatenate(
        [
            jnp.concatenate([square[: K // 2], square[K // 2 :]], axis=1),
            jnp.broadcast_to(jnp.concatenate([diag, diag])[None], (8, 2 * K)),
        ],
        axis=0,
    )
    over_y = lax.all_to_all(
        spread(jnp.concatenate([packed, my_query], axis=0), NY),
        "dp", 0, 0, axis_index_groups=Y_GROUPS,
    )
    packed = over_y[:, :40].sum(0)
    my_queries = over_y[:, 40:]
    packed = lax.all_to_all(spread(packed, NZ), "dp", 0, 0, axis_index_groups=Z_GROUPS).sum(0)
    in_ex = in_proj.reshape(EX_DEV, TOK_EX, K)
    out_ex = out_proj.reshape(EX_DEV, TOK_EX, K)
    example_grads = jnp.einsum("eti,eto->eio", in_ex, out_ex, precision=lax.Precision.HIGHEST)
    example_grads = example_grads / math.sqrt(TOK_EX)
    square = jnp.concatenate([packed[:32, :K], packed[:32, K:]], axis=0)
    low = jnp.where(rows >= cols, square, 0.0)
    high = jnp.where(rows < cols, square, 0.0)
    sum_in = jnp.where(rows >= cols, square, low.T)
    sum_out = high + high.T + eye_mat * packed[32, :K]
    factor_in = sum_in / all_tokens + damping_level * eye_mat
    factor_out = sum_out / all_tokens + damping_level * eye_mat
    chol_in = jnp.linalg.cholesky(factor_in)
    chol_out = jnp.linalg.cholesky(factor_out)
    left = jax.scipy.linalg.cho_solve(
        (chol_in, True), example_grads.transpose(1, 0, 2).reshape(K, EX_DEV * K)
    )
    left = left.reshape(K, EX_DEV, K).transpose(2, 1, 0).reshape(K, EX_DEV * K)
    right = jax.scipy.linalg.cho_solve((chol_out, True), left)
    ready = right.reshape(K, EX_DEV, K).transpose(1, 2, 0).reshape(EX_DEV, K * K)
    part_scores = jnp.dot(
        ready, my_queries.reshape(NY, K * K).T, precision=lax.Precision.HIGHEST
    ) / float(K)
    scores = lax.all_to_all(spread(part_scores, NT), "tensor", 0, 0)
    scores = scores.transpose(1, 2, 0).reshape(EX_DEV, NY * NT)
    return (example_grads.reshape(EX_DEV, K * K), factor_in, factor_out, scores)


def solution(mesh):
    placed = (
        P("dp", "tensor"),
        P("dp", "tensor"),
        P("tensor", None),
        P("tensor", None),
        P("dp", None),
    )
    return jax.shard_map(
        local,
        mesh=mesh,
        in_specs=placed,
        out_specs=(P("dp", None), P(), P(), P("dp", None)),
        check_vma=False,
    )
```

```python
import functools
import math

import jax
import jax.numpy as jnp
from jax import lax
from jax.experimental import pallas as pl
from jax.experimental.pallas import tpu as pltpu
from jax.sharding import PartitionSpec as P

EX_DEV = 4
TOK_EX = 112
K = 64
NQ = 64
NY = 8
NZ = 8
NT = 8
GRAM = 40
ROWS = 56
QROWS = 32
UNIT_BLOCKS = (1280, 1280, 1024)
HI = lax.Precision.HIGHEST
F32 = jnp.float32
VMEM_LIMIT = 16 << 20
WIDE_VMEM_LIMIT = 60 << 20


damping_level = 0.1

Y_GROUPS = [[y * NZ + z for y in range(NY)] for z in range(NZ)]
Z_GROUPS = [[y * NZ + z for z in range(NZ)] for y in range(NY)]


def swap_pairs():
    pairs = []
    for y in range(NY):
        for z in range(NZ):
            for t in range(NT):
                pairs.append(((y * NZ + z) * NT + t, (y * NZ + t) * NT + z))
    return pairs


def gauss_jordan(m, panel):
    lane = lax.broadcasted_iota(jnp.int32, (K, 2 * K), 1)
    half = lane & K
    col_of = lane & (K - 1)
    sub = lax.broadcasted_iota(jnp.int32, (K, 2 * K), 0)
    for first in range(0, K, panel):
        cols = [jnp.take_along_axis(m, half + k, axis=1) for k in range(first, first + panel)]
        for k in range(first, first + panel):
            c = cols[k - first]
            inv = 1.0 / c[k : k + 1]
            row = jnp.where(col_of[:1] == k, 1.0, m[k : k + 1]) * inv
            for j in range(k + 1, first + panel):
                d = cols[j - first]
                f = d[k : k + 1] * inv
                cols[j - first] = jnp.where(sub == k, f, d - c * f)
            m = jnp.where(sub == k, row, jnp.where(col_of == k, 0.0, m) - c * row)
    return m


def call(body, outs, *args, scratch=(), flops=1 << 20):
    return pl.pallas_call(
        body,
        out_shape=[jax.ShapeDtypeStruct(shape, F32) for shape in outs],
        scratch_shapes=[pltpu.VMEM(shape, F32) for shape in scratch],
        compiler_params=pltpu.CompilerParams(vmem_limit_bytes=VMEM_LIMIT),
        cost_estimate=pl.CostEstimate(flops=flops, bytes_accessed=1 << 20, transcendentals=0),
    )(*args)


def added(ref, rows):
    total = ref[0, rows]
    for i in range(1, ref.shape[0]):
        total = total + ref[i, rows]
    return total


def project_kernel(hidden_ref, grad_ref, win_ref, wout_ref, out_ref, hidden, grad, win, wout, sems):
    contract = (((1,), (1,)), ((), ()))
    wout_copy = pltpu.make_async_copy(wout_ref, wout, sems.at[0])
    grad_copy = pltpu.make_async_copy(grad_ref, grad, sems.at[1])
    win_copy = pltpu.make_async_copy(win_ref, win, sems.at[2])
    wout_copy.start()
    grad_copy.start()
    win_copy.start()
    blocks = []
    first = 0
    for i, size in enumerate(UNIT_BLOCKS):
        units = pl.ds(first, size)
        copy = pltpu.make_async_copy(hidden_ref.at[:, units], hidden.at[:, units], sems.at[3 + i])
        copy.start()
        blocks.append((copy, units))
        first += size
    wout_copy.wait()
    grad_copy.wait()
    out_part = lax.dot_general(grad[...], wout[...], contract, preferred_element_type=F32)
    win_copy.wait()
    in_part = None
    for copy, units in blocks:
        copy.wait()
        part = lax.dot_general(hidden[:, units], win[:, units], contract, preferred_element_type=F32)
        in_part = part if in_part is None else in_part + part
    out_ref[:, :, :K] = in_part.reshape(NT, ROWS, K)
    out_ref[:, :, K:] = out_part.reshape(NT, ROWS, K)


def project(hidden_act, grad_out, proj_in, proj_out):
    operands = (hidden_act, grad_out, proj_in.T, proj_out.T)
    return pl.pallas_call(
        project_kernel,
        in_specs=[pl.BlockSpec(memory_space=pltpu.HBM)] * len(operands),
        out_shape=jax.ShapeDtypeStruct((NT, ROWS, 2 * K), F32),
        scratch_shapes=[pltpu.VMEM(x.shape, x.dtype) for x in operands]
        + [pltpu.SemaphoreType.DMA((3 + len(UNIT_BLOCKS),))],
        compiler_params=pltpu.CompilerParams(vmem_limit_bytes=WIDE_VMEM_LIMIT),
    )(*operands)


def rows_kernel(parts_ref, query_ref, send_ref, kept_ref):
    mine = added(parts_ref, pl.ds(0, ROWS))
    for t in range(NT):
        send_ref[t] = mine
    kept_ref[...] = query_ref[...]


def gram_kernel(rows_ref, query_ref, send_ref, wide_ref):
    gram = jnp.zeros((2 * K, 2 * K), F32)
    for e in range(EX_DEV):
        rows = rows_ref[2 * e : 2 * e + 2].reshape(TOK_EX, 2 * K)
        product = lax.dot_general(
            rows, rows, (((0,), (0,)), ((), ())), precision=HI, preferred_element_type=F32
        )
        gram = gram + product
        pair, side = divmod(e, 2)
        grad = product[:K, K:] / math.sqrt(TOK_EX)
        wide_ref[pair * K : (pair + 1) * K, side * K : (side + 1) * K] = grad
    packed = pack(gram[:K, :K], gram[K:, K:])
    query = query_ref[...]
    for y in range(NY):
        send_ref[y, :GRAM] = packed
        send_ref[y, GRAM:] = query


def over_y_kernel(parts_ref, send_ref):
    packed = added(parts_ref, pl.ds(0, GRAM))
    for z in range(NZ):
        send_ref[z] = packed


def pack(square_in, square_out):
    rows = lax.broadcasted_iota(jnp.int32, (K, K), 0)
    cols = lax.broadcasted_iota(jnp.int32, (K, K), 1)
    square = jnp.where(rows >= cols, square_in, square_out)
    diag = jnp.sum(jnp.where(rows == cols, square_out, 0.0), axis=0, keepdims=True)
    diag = jnp.broadcast_to(jnp.concatenate([diag, diag], axis=1), (8, 2 * K))
    return jnp.concatenate(
        [jnp.concatenate([square[: K // 2], square[K // 2 :]], axis=1), diag], axis=0
    )

def unpack(packed):
    rows = lax.broadcasted_iota(jnp.int32, (K, K), 0)
    cols = lax.broadcasted_iota(jnp.int32, (K, K), 1)
    square = jnp.concatenate([packed[: K // 2, :K], packed[: K // 2, K:]], axis=0)
    flipped = square.T
    square_in = jnp.where(rows >= cols, square, flipped)
    square_out = jnp.where(rows < cols, square, flipped)
    square_out = jnp.where(rows == cols, packed[K // 2 : K // 2 + 1, :K], square_out)
    return square_in, square_out

def wide_rows(wide_ref):
    blocks = []
    for pair in range(2):
        even = wide_ref[pl.ds(pair * K, K // 2, stride=2), :]
        odd = wide_ref[pl.ds(pair * K + 1, K // 2, stride=2), :]
        blocks.append(jnp.concatenate([even[:, :K], odd[:, :K]], axis=1))
        blocks.append(jnp.concatenate([even[:, K:], odd[:, K:]], axis=1))
    return blocks


def tail_kernel(all_tokens, parts_ref, grads_ref, query_ref, factors_ref, send_ref, wide_ref):
    sum_in, sum_out = unpack(added(parts_ref, pl.ds(0, GRAM)))
    rows = lax.broadcasted_iota(jnp.int32, (K, 2 * K), 0)
    cols = lax.broadcasted_iota(jnp.int32, (K, 2 * K), 1)
    eye_mats = jnp.where(rows == (cols & (K - 1)), 1.0, 0.0)
    factors = jnp.concatenate([sum_in, sum_out], axis=1) / all_tokens + damping_level * eye_mats
    factors_ref[...] = factors
    inverse = gauss_jordan(factors, 8)
    in_inv = inverse[:, :K]
    out_inv = inverse[:, K:] / float(K)
    zero = jnp.zeros((K, K), F32)
    pair_inv = jnp.concatenate(
        [jnp.concatenate([out_inv, zero], axis=1), jnp.concatenate([zero, out_inv], axis=1)], axis=0
    )
    for pair in range(2):
        left = jnp.dot(
            in_inv, grads_ref[pair * K : (pair + 1) * K], precision=HI, preferred_element_type=F32
        )
        wide_ref[pair * K : (pair + 1) * K] = jnp.dot(
            left, pair_inv, precision=HI, preferred_element_type=F32
        )
    ready = wide_rows(wide_ref)
    sums = [jnp.zeros((NY, 2 * K), F32) for _ in range(EX_DEV)]
    for r in range(QROWS):
        block = query_ref[pl.ds(GRAM + r, NY, stride=GRAM + QROWS), :]
        for e in range(EX_DEV):
            sums[e] = sums[e] + block * ready[e][r : r + 1]
    total = lax.dot_general(
        jnp.ones((8, 2 * K), F32),
        jnp.concatenate(sums, axis=0),
        (((1,), (1,)), ((), ())),
        precision=HI,
        preferred_element_type=F32,
    )
    source = lax.broadcasted_iota(jnp.int32, (EX_DEV * NY, EX_DEV * NQ), 0)
    target = lax.broadcasted_iota(jnp.int32, (EX_DEV * NY, EX_DEV * NQ), 1)
    place = jnp.where(source * NZ + lax.axis_index("tensor") == target, 1.0, 0.0)
    placed = jnp.dot(total, place, precision=HI, preferred_element_type=F32)
    for t in range(NT):
        send_ref[t] = placed[:1]


def last_kernel(parts_ref, factors_ref, wide_ref, grads_ref, fin_ref, fout_ref, scores_ref, tall_ref):
    total = added(parts_ref, pl.ds(0, 1))
    for e in range(EX_DEV):
        scores_ref[e : e + 1, :] = total[:, e * NQ : (e + 1) * NQ]
    fin_ref[...] = factors_ref[:, :K]
    fout_ref[...] = factors_ref[:, K:]
    for e, block in enumerate(wide_rows(wide_ref)):
        tall_ref[e * QROWS : (e + 1) * QROWS] = block
    for r in range(QROWS):
        grads_ref[:, r * 2 * K : (r + 1) * 2 * K] = tall_ref[pl.ds(r, EX_DEV, stride=QROWS), :]


def local(hidden_act, grad_out, proj_in, proj_out, queries):
    all_tokens = float(hidden_act.shape[0] * lax.axis_size("dp"))
    query = lax.ppermute(queries.reshape(QROWS, 2 * K), ("dp", "tensor"), swap_pairs())
    part = project(hidden_act, grad_out, proj_in, proj_out)
    parts = lax.all_to_all(part, "tensor", 0, 0)
    send, query = call(rows_kernel, [(NT, ROWS, 2 * K), (QROWS, 2 * K)], parts, query)
    rows = lax.all_to_all(send, "tensor", 0, 0)
    send, wide = call(gram_kernel, [(NY, GRAM + QROWS, 2 * K), (2 * K, 2 * K)], rows, query)
    over_y = lax.all_to_all(send, "dp", 0, 0, axis_index_groups=Y_GROUPS)
    (send,) = call(over_y_kernel, [(NZ, GRAM, 2 * K)], over_y)
    parts = lax.all_to_all(send, "dp", 0, 0, axis_index_groups=Z_GROUPS)
    factors, send = call(
        functools.partial(tail_kernel, all_tokens),
        [(K, 2 * K), (NT, 1, EX_DEV * NQ)],
        parts,
        wide,
        over_y.reshape(NY * (GRAM + QROWS), 2 * K),
        scratch=[(2 * K, 2 * K)],
    )
    parts = lax.all_to_all(send, "tensor", 0, 0)
    return tuple(
        call(
            last_kernel,
            [(EX_DEV, K * K), (K, K), (K, K), (EX_DEV, NQ)],
            parts,
            factors,
            wide,
            scratch=[(EX_DEV * QROWS, 2 * K)],
        )
    )


def solution(mesh):
    placed = (
        P("dp", "tensor"),
        P("dp", "tensor"),
        P("tensor", None),
        P("tensor", None),
        P("dp", None),
    )
    return jax.shard_map(
        local,
        mesh=mesh,
        in_specs=placed,
        out_specs=(P("dp", None), P(), P(), P("dp", None)),
        check_vma=False,
    )
```

```python
import functools
import math

import jax
import jax.numpy as jnp
from jax import lax
from jax.experimental import pallas as pl
from jax.experimental.pallas import tpu as pltpu
from jax.sharding import PartitionSpec as P

EX_DEV = 4
TOK_EX = 112
K = 64
NQ = 64
NY = 8
NZ = 8
NT = 8
GRAM = 40
ROWS = 56
QROWS = 32
SLICE = QROWS // NT
UNIT_BLOCKS = (1280, 1280, 1024)
HI = lax.Precision.HIGHEST
F32 = jnp.float32
VMEM_LIMIT = 16 << 20
WIDE_VMEM_LIMIT = 60 << 20


damping_level = 0.1

Y_GROUPS = [[y * NZ + z for y in range(NY)] for z in range(NZ)]
Z_GROUPS = [[y * NZ + z for z in range(NZ)] for y in range(NY)]


def gauss_jordan(m, panel):
    lane = lax.broadcasted_iota(jnp.int32, (K, 2 * K), 1)
    half = lane & K
    col_of = lane & (K - 1)
    sub = lax.broadcasted_iota(jnp.int32, (K, 2 * K), 0)
    for first in range(0, K, panel):
        cols = [jnp.take_along_axis(m, half + k, axis=1) for k in range(first, first + panel)]
        for k in range(first, first + panel):
            c = cols[k - first]
            inv = 1.0 / c[k : k + 1]
            row = jnp.where(col_of[:1] == k, 1.0, m[k : k + 1]) * inv
            for j in range(k + 1, first + panel):
                d = cols[j - first]
                f = d[k : k + 1] * inv
                cols[j - first] = jnp.where(sub == k, f, d - c * f)
            m = jnp.where(sub == k, row, jnp.where(col_of == k, 0.0, m) - c * row)
    return m


def call(body, outs, *args, scratch=(), flops=1 << 20):
    return pl.pallas_call(
        body,
        out_shape=[jax.ShapeDtypeStruct(shape, F32) for shape in outs],
        scratch_shapes=[pltpu.VMEM(shape, F32) for shape in scratch],
        compiler_params=pltpu.CompilerParams(vmem_limit_bytes=VMEM_LIMIT),
        cost_estimate=pl.CostEstimate(flops=flops, bytes_accessed=1 << 20, transcendentals=0),
    )(*args)


def added(ref, rows):
    total = ref[0, rows]
    for i in range(1, ref.shape[0]):
        total = total + ref[i, rows]
    return total


def project_kernel(hidden_ref, grad_ref, win_ref, wout_ref, out_ref, hidden, grad, win, wout, sems):
    contract = (((1,), (1,)), ((), ()))
    wout_copy = pltpu.make_async_copy(wout_ref, wout, sems.at[0])
    grad_copy = pltpu.make_async_copy(grad_ref, grad, sems.at[1])
    win_copy = pltpu.make_async_copy(win_ref, win, sems.at[2])
    wout_copy.start()
    grad_copy.start()
    win_copy.start()
    blocks = []
    first = 0
    for i, size in enumerate(UNIT_BLOCKS):
        units = pl.ds(first, size)
        copy = pltpu.make_async_copy(hidden_ref.at[:, units], hidden.at[:, units], sems.at[3 + i])
        copy.start()
        blocks.append((copy, units))
        first += size
    wout_copy.wait()
    grad_copy.wait()
    out_part = lax.dot_general(grad[...], wout[...], contract, preferred_element_type=F32)
    win_copy.wait()
    in_part = None
    for copy, units in blocks:
        copy.wait()
        part = lax.dot_general(hidden[:, units], win[:, units], contract, preferred_element_type=F32)
        in_part = part if in_part is None else in_part + part
    out_ref[:, :, :K] = in_part.reshape(NT, ROWS, K)
    out_ref[:, :, K:] = out_part.reshape(NT, ROWS, K)


def project(hidden_act, grad_out, proj_in, proj_out):
    operands = (hidden_act, grad_out, proj_in.T, proj_out.T)
    return pl.pallas_call(
        project_kernel,
        in_specs=[pl.BlockSpec(memory_space=pltpu.HBM)] * len(operands),
        out_shape=jax.ShapeDtypeStruct((NT, ROWS, 2 * K), F32),
        scratch_shapes=[pltpu.VMEM(x.shape, x.dtype) for x in operands]
        + [pltpu.SemaphoreType.DMA((3 + len(UNIT_BLOCKS),))],
        compiler_params=pltpu.CompilerParams(vmem_limit_bytes=WIDE_VMEM_LIMIT),
    )(*operands)


def rows_kernel(parts_ref, send_ref):
    mine = added(parts_ref, pl.ds(0, ROWS))
    for t in range(NT):
        send_ref[t] = mine


def gram_kernel(rows_ref, query_ref, send_ref, wide_ref):
    gram = jnp.zeros((2 * K, 2 * K), F32)
    for e in range(EX_DEV):
        rows = rows_ref[2 * e : 2 * e + 2].reshape(TOK_EX, 2 * K)
        product = lax.dot_general(
            rows, rows, (((0,), (0,)), ((), ())), precision=HI, preferred_element_type=F32
        )
        gram = gram + product
        pair, side = divmod(e, 2)
        grad = product[:K, K:] / math.sqrt(TOK_EX)
        wide_ref[pair * K : (pair + 1) * K, side * K : (side + 1) * K] = grad
    query = query_ref[lax.axis_index("tensor")]
    packed = pack(gram[:K, :K], gram[K:, K:], query)
    for z in range(NZ):
        send_ref[z] = packed


def over_z_kernel(parts_ref, send_ref):
    packed = added(parts_ref, pl.ds(0, GRAM))
    queries = jnp.concatenate([parts_ref[z, GRAM - SLICE :] for z in range(NZ)], axis=0)
    for y in range(NY):
        send_ref[y, :GRAM] = packed
        send_ref[y, GRAM:] = queries


def pack(square_in, square_out, query):
    rows = lax.broadcasted_iota(jnp.int32, (K, K), 0)
    cols = lax.broadcasted_iota(jnp.int32, (K, K), 1)
    square = jnp.where(rows >= cols, square_in, square_out)
    diag = jnp.sum(jnp.where(rows == cols, square_out, 0.0), axis=0, keepdims=True)
    diag = jnp.broadcast_to(jnp.concatenate([diag, diag], axis=1), (SLICE, 2 * K))
    return jnp.concatenate(
        [jnp.concatenate([square[: K // 2], square[K // 2 :]], axis=1), diag, query], axis=0
    )

def unpack(packed):
    rows = lax.broadcasted_iota(jnp.int32, (K, K), 0)
    cols = lax.broadcasted_iota(jnp.int32, (K, K), 1)
    square = jnp.concatenate([packed[: K // 2, :K], packed[: K // 2, K:]], axis=0)
    flipped = square.T
    square_in = jnp.where(rows >= cols, square, flipped)
    square_out = jnp.where(rows < cols, square, flipped)
    square_out = jnp.where(rows == cols, packed[K // 2 : K // 2 + 1, :K], square_out)
    return square_in, square_out

def wide_rows(wide_ref, count):
    blocks = []
    for pair in range(2):
        even = wide_ref[pl.ds(pair * count, count // 2, stride=2), :]
        odd = wide_ref[pl.ds(pair * count + 1, count // 2, stride=2), :]
        blocks.append(jnp.concatenate([even[:, :K], odd[:, :K]], axis=1))
        blocks.append(jnp.concatenate([even[:, K:], odd[:, K:]], axis=1))
    return blocks


def tail_kernel(all_tokens, parts_ref, grads_ref, factors_ref, send_ref, inverse_ref, wide_ref):
    sum_in, sum_out = unpack(added(parts_ref, pl.ds(0, GRAM)))
    rows = lax.broadcasted_iota(jnp.int32, (K, 2 * K), 0)
    cols = lax.broadcasted_iota(jnp.int32, (K, 2 * K), 1)
    eye_mats = jnp.where(rows == (cols & (K - 1)), 1.0, 0.0)
    factors = jnp.concatenate([sum_in, sum_out], axis=1) / all_tokens + damping_level * eye_mats
    factors_ref[...] = factors
    inverse = gauss_jordan(factors, 8)
    inverse_ref[...] = inverse
    count = 2 * SLICE
    mine = inverse_ref[pl.ds(pl.multiple_of(lax.axis_index("tensor") * count, count), count), :]
    out_inv = inverse[:, K:] / float(K)
    zero = jnp.zeros((K, K), F32)
    pair_inv = jnp.concatenate(
        [jnp.concatenate([out_inv, zero], axis=1), jnp.concatenate([zero, out_inv], axis=1)], axis=0
    )
    left = [
        jnp.dot(
            mine[:, :K],
            grads_ref[pair * K : (pair + 1) * K],
            precision=HI,
            preferred_element_type=F32,
        )
        for pair in range(2)
    ]
    wide_ref[...] = jnp.dot(
        jnp.concatenate(left, axis=0), pair_inv, precision=HI, preferred_element_type=F32
    )
    ready = wide_rows(wide_ref, count)
    sums = [[] for _ in range(EX_DEV)]
    for y in range(NY):
        blocks = [parts_ref[y, pl.ds(GRAM + r, NZ, stride=SLICE), :] for r in range(SLICE)]
        for e in range(EX_DEV):
            total = blocks[0] * ready[e][:1]
            for r in range(1, SLICE):
                total = total + blocks[r] * ready[e][r : r + 1]
            sums[e].append(total)
    scores = lax.dot_general(
        jnp.ones((8, 2 * K), F32),
        jnp.concatenate([total for part in sums for total in part], axis=0),
        (((1,), (1,)), ((), ())),
        precision=HI,
        preferred_element_type=F32,
    )
    for t in range(NT):
        send_ref[t] = scores[:1]


def last_kernel(parts_ref, factors_ref, wide_ref, grads_ref, fin_ref, fout_ref, scores_ref, tall_ref):
    total = added(parts_ref, pl.ds(0, 1))
    for e in range(EX_DEV):
        scores_ref[e : e + 1, :] = total[:, e * NQ : (e + 1) * NQ]
    fin_ref[...] = factors_ref[:, :K]
    fout_ref[...] = factors_ref[:, K:]
    for e, block in enumerate(wide_rows(wide_ref, K)):
        tall_ref[e * QROWS : (e + 1) * QROWS] = block
    for r in range(QROWS):
        grads_ref[:, r * 2 * K : (r + 1) * 2 * K] = tall_ref[pl.ds(r, EX_DEV, stride=QROWS), :]


def local(hidden_act, grad_out, proj_in, proj_out, queries):
    all_tokens = float(hidden_act.shape[0] * lax.axis_size("dp"))
    part = project(hidden_act, grad_out, proj_in, proj_out)
    parts = lax.all_to_all(part, "tensor", 0, 0)
    (send,) = call(rows_kernel, [(NT, ROWS, 2 * K)], parts)
    rows = lax.all_to_all(send, "tensor", 0, 0)
    send, wide = call(
        gram_kernel,
        [(NZ, GRAM, 2 * K), (2 * K, 2 * K)],
        rows,
        queries.reshape(NT, SLICE, 2 * K),
    )
    parts = lax.all_to_all(send, "dp", 0, 0, axis_index_groups=Z_GROUPS)
    (send,) = call(over_z_kernel, [(NY, GRAM + QROWS, 2 * K)], parts)
    parts = lax.all_to_all(send, "dp", 0, 0, axis_index_groups=Y_GROUPS)
    factors, send = call(
        functools.partial(tail_kernel, all_tokens),
        [(K, 2 * K), (NT, 1, EX_DEV * NQ)],
        parts,
        wide,
        scratch=[(K, 2 * K), (4 * SLICE, 2 * K)],
    )
    parts = lax.all_to_all(send, "tensor", 0, 0)
    return tuple(
        call(
            last_kernel,
            [(EX_DEV, K * K), (K, K), (K, K), (EX_DEV, NQ)],
            parts,
            factors,
            wide,
            scratch=[(EX_DEV * QROWS, 2 * K)],
        )
    )


def solution(mesh):
    placed = (
        P("dp", "tensor"),
        P("dp", "tensor"),
        P("tensor", None),
        P("tensor", None),
        P("dp", None),
    )
    return jax.shard_map(
        local,
        mesh=mesh,
        in_specs=placed,
        out_specs=(P("dp", None), P(), P(), P("dp", None)),
        check_vma=False,
    )
```

```python
import functools
import math

import jax
import jax.numpy as jnp
from jax import lax
from jax.experimental import pallas as pl
from jax.experimental.pallas import tpu as pltpu
from jax.sharding import PartitionSpec as P

EX_DEV = 4
TOK_EX = 112
K = 64
NQ = 64
NY = 8
NZ = 8
NT = 8
GRAM = 40
ROWS = 56
QROWS = 32
SLICE = QROWS // NT
UNIT_BLOCKS = (1280, 1280, 1024)
HI = lax.Precision.HIGHEST
F32 = jnp.float32
VMEM_LIMIT = 16 << 20
WIDE_VMEM_LIMIT = 60 << 20


damping_level = 0.1

Y_GROUPS = [[y * NZ + z for y in range(NY)] for z in range(NZ)]
Z_GROUPS = [[y * NZ + z for z in range(NZ)] for y in range(NY)]


def ldl_inverse(m):
    count = K // 8
    tiles = [m[8 * i : 8 * i + 8] for i in range(count)]
    lane = lax.broadcasted_iota(jnp.int32, (8, 2 * K), 1)
    half = lane & K
    col_of = lane & (K - 1)
    sub = lax.broadcasted_iota(jnp.int32, (8, 2 * K), 0)
    unit, scaled = [], []
    for p in range(count):
        below = range(p, count)
        cols = [
            {t: jnp.take_along_axis(tiles[t], half + (8 * p + s), axis=1) for t in below}
            for s in range(8)
        ]
        inside = (col_of & -8) == 8 * p
        for t in below:
            tiles[t] = jnp.where(inside, 0.0, tiles[t])
        inverses = []
        for s in range(8):
            c = cols[s]
            inv = 1.0 / c[p][s : s + 1]
            inverses.append(inv)
            for j in range(s + 1, 8):
                d = cols[j]
                f = d[p][s : s + 1] * inv
                cols[j] = {t: d[t] - c[t] * f for t in below}
            row = jnp.where(col_of[:1] == 8 * p + s, 1.0, tiles[p][s : s + 1]) * inv
            for t in below:
                new = tiles[t] - c[t] * row
                tiles[t] = jnp.where(sub > s, new, tiles[t]) if t == p else new
        lower = jnp.where(col_of < 8 * p + sub, tiles[p], jnp.where(col_of == 8 * p + sub, 1.0, 0.0))
        unit.append(lower)
        scaled.append(lower * jnp.concatenate(inverses, axis=0))
    both = lax.dot_general(
        jnp.concatenate(unit, axis=0),
        jnp.concatenate(scaled, axis=0),
        (((0,), (0,)), ((), ())),
        precision=HI,
        preferred_element_type=F32,
    )
    return jnp.concatenate([both[:K, :K], both[K:, K:]], axis=1)


def call(body, outs, *args, scratch=(), flops=1 << 20):
    return pl.pallas_call(
        body,
        out_shape=[jax.ShapeDtypeStruct(shape, F32) for shape in outs],
        scratch_shapes=[pltpu.VMEM(shape, F32) for shape in scratch],
        compiler_params=pltpu.CompilerParams(vmem_limit_bytes=VMEM_LIMIT),
        cost_estimate=pl.CostEstimate(flops=flops, bytes_accessed=1 << 20, transcendentals=0),
    )(*args)


def added(ref, rows):
    total = ref[0, rows]
    for i in range(1, ref.shape[0]):
        total = total + ref[i, rows]
    return total


def project_kernel(hidden_ref, grad_ref, win_ref, wout_ref, out_ref, hidden, grad, win, wout, sems):
    contract = (((1,), (1,)), ((), ()))
    wout_copy = pltpu.make_async_copy(wout_ref, wout, sems.at[0])
    grad_copy = pltpu.make_async_copy(grad_ref, grad, sems.at[1])
    win_copy = pltpu.make_async_copy(win_ref, win, sems.at[2])
    wout_copy.start()
    grad_copy.start()
    win_copy.start()
    blocks = []
    first = 0
    for i, size in enumerate(UNIT_BLOCKS):
        units = pl.ds(first, size)
        copy = pltpu.make_async_copy(hidden_ref.at[:, units], hidden.at[:, units], sems.at[3 + i])
        copy.start()
        blocks.append((copy, units))
        first += size
    wout_copy.wait()
    grad_copy.wait()
    out_part = lax.dot_general(wout[...], grad[...], contract, preferred_element_type=F32)
    win_copy.wait()
    in_part = None
    for copy, units in blocks:
        copy.wait()
        part = lax.dot_general(win[:, units], hidden[:, units], contract, preferred_element_type=F32)
        in_part = part if in_part is None else in_part + part
    out_ref[...] = jnp.concatenate([in_part, out_part], axis=0).T.reshape(NT, ROWS, 2 * K)


def project(hidden_act, grad_out, proj_in, proj_out):
    operands = (hidden_act, grad_out, proj_in.T, proj_out.T)
    return pl.pallas_call(
        project_kernel,
        in_specs=[pl.BlockSpec(memory_space=pltpu.HBM)] * len(operands),
        out_shape=jax.ShapeDtypeStruct((NT, ROWS, 2 * K), F32),
        scratch_shapes=[pltpu.VMEM(x.shape, x.dtype) for x in operands]
        + [pltpu.SemaphoreType.DMA((3 + len(UNIT_BLOCKS),))],
        compiler_params=pltpu.CompilerParams(vmem_limit_bytes=WIDE_VMEM_LIMIT),
    )(*operands)


def rows_kernel(parts_ref, send_ref):
    mine = added(parts_ref, pl.ds(0, ROWS))
    for t in range(NT):
        send_ref[t] = mine


def gram_kernel(rows_ref, query_ref, send_ref, wide_ref):
    gram = jnp.zeros((2 * K, 2 * K), F32)
    for e in range(EX_DEV):
        rows = rows_ref[2 * e : 2 * e + 2].reshape(TOK_EX, 2 * K)
        product = lax.dot_general(
            rows, rows, (((0,), (0,)), ((), ())), precision=HI, preferred_element_type=F32
        )
        gram = gram + product
        pair, side = divmod(e, 2)
        grad = product[:K, K:] / math.sqrt(TOK_EX)
        wide_ref[pair * K : (pair + 1) * K, side * K : (side + 1) * K] = grad
    query = query_ref[lax.axis_index("tensor")]
    packed = pack(gram[:K, :K], gram[K:, K:], query)
    for z in range(NZ):
        send_ref[z] = packed


def over_z_kernel(parts_ref, send_ref):
    packed = added(parts_ref, pl.ds(0, GRAM))
    queries = jnp.concatenate([parts_ref[z, GRAM - SLICE :] for z in range(NZ)], axis=0)
    for y in range(NY):
        send_ref[y, :GRAM] = packed
        send_ref[y, GRAM:] = queries


def pack(square_in, square_out, query):
    rows = lax.broadcasted_iota(jnp.int32, (K, K), 0)
    cols = lax.broadcasted_iota(jnp.int32, (K, K), 1)
    square = jnp.where(rows >= cols, square_in, square_out)
    diag = jnp.sum(jnp.where(rows == cols, square_out, 0.0), axis=0, keepdims=True)
    diag = jnp.broadcast_to(jnp.concatenate([diag, diag], axis=1), (SLICE, 2 * K))
    return jnp.concatenate(
        [jnp.concatenate([square[: K // 2], square[K // 2 :]], axis=1), diag, query], axis=0
    )

def unpack(packed):
    rows = lax.broadcasted_iota(jnp.int32, (K, K), 0)
    cols = lax.broadcasted_iota(jnp.int32, (K, K), 1)
    square = jnp.concatenate([packed[: K // 2, :K], packed[: K // 2, K:]], axis=0)
    flipped = square.T
    square_in = jnp.where(rows >= cols, square, flipped)
    square_out = jnp.where(rows < cols, square, flipped)
    square_out = jnp.where(rows == cols, packed[K // 2 : K // 2 + 1, :K], square_out)
    return square_in, square_out

def wide_rows(wide_ref, count):
    blocks = []
    for pair in range(2):
        even = wide_ref[pl.ds(pair * count, count // 2, stride=2), :]
        odd = wide_ref[pl.ds(pair * count + 1, count // 2, stride=2), :]
        blocks.append(jnp.concatenate([even[:, :K], odd[:, :K]], axis=1))
        blocks.append(jnp.concatenate([even[:, K:], odd[:, K:]], axis=1))
    return blocks


def tail_kernel(all_tokens, parts_ref, grads_ref, factors_ref, send_ref, inverse_ref, wide_ref):
    sum_in, sum_out = unpack(added(parts_ref, pl.ds(0, GRAM)))
    rows = lax.broadcasted_iota(jnp.int32, (K, 2 * K), 0)
    cols = lax.broadcasted_iota(jnp.int32, (K, 2 * K), 1)
    eye_mats = jnp.where(rows == (cols & (K - 1)), 1.0, 0.0)
    factors = jnp.concatenate([sum_in, sum_out], axis=1) / all_tokens + damping_level * eye_mats
    factors_ref[...] = factors
    inverse = ldl_inverse(factors)
    inverse_ref[...] = inverse
    count = 2 * SLICE
    mine = inverse_ref[pl.ds(pl.multiple_of(lax.axis_index("tensor") * count, count), count), :]
    out_inv = inverse[:, K:] / float(K)
    zero = jnp.zeros((K, K), F32)
    pair_inv = jnp.concatenate(
        [jnp.concatenate([out_inv, zero], axis=1), jnp.concatenate([zero, out_inv], axis=1)], axis=0
    )
    left = [
        jnp.dot(
            mine[:, :K],
            grads_ref[pair * K : (pair + 1) * K],
            precision=HI,
            preferred_element_type=F32,
        )
        for pair in range(2)
    ]
    wide_ref[...] = jnp.dot(
        jnp.concatenate(left, axis=0), pair_inv, precision=HI, preferred_element_type=F32
    )
    ready = wide_rows(wide_ref, count)
    sums = [[] for _ in range(EX_DEV)]
    for y in range(NY):
        blocks = [parts_ref[y, pl.ds(GRAM + r, NZ, stride=SLICE), :] for r in range(SLICE)]
        for e in range(EX_DEV):
            total = blocks[0] * ready[e][:1]
            for r in range(1, SLICE):
                total = total + blocks[r] * ready[e][r : r + 1]
            sums[e].append(total)
    scores = lax.dot_general(
        jnp.ones((8, 2 * K), F32),
        jnp.concatenate([total for part in sums for total in part], axis=0),
        (((1,), (1,)), ((), ())),
        precision=HI,
        preferred_element_type=F32,
    )
    for t in range(NT):
        send_ref[t] = scores[:1]


def last_kernel(parts_ref, factors_ref, wide_ref, grads_ref, fin_ref, fout_ref, scores_ref, tall_ref):
    total = added(parts_ref, pl.ds(0, 1))
    for e in range(EX_DEV):
        scores_ref[e : e + 1, :] = total[:, e * NQ : (e + 1) * NQ]
    fin_ref[...] = factors_ref[:, :K]
    fout_ref[...] = factors_ref[:, K:]
    for e, block in enumerate(wide_rows(wide_ref, K)):
        tall_ref[e * QROWS : (e + 1) * QROWS] = block
    for r in range(QROWS):
        grads_ref[:, r * 2 * K : (r + 1) * 2 * K] = tall_ref[pl.ds(r, EX_DEV, stride=QROWS), :]


def local(hidden_act, grad_out, proj_in, proj_out, queries):
    all_tokens = float(hidden_act.shape[0] * lax.axis_size("dp"))
    part = project(hidden_act, grad_out, proj_in, proj_out)
    parts = lax.all_to_all(part, "tensor", 0, 0)
    (send,) = call(rows_kernel, [(NT, ROWS, 2 * K)], parts)
    rows = lax.all_to_all(send, "tensor", 0, 0)
    send, wide = call(
        gram_kernel,
        [(NZ, GRAM, 2 * K), (2 * K, 2 * K)],
        rows,
        queries.reshape(NT, SLICE, 2 * K),
    )
    parts = lax.all_to_all(send, "dp", 0, 0, axis_index_groups=Z_GROUPS)
    (send,) = call(over_z_kernel, [(NY, GRAM + QROWS, 2 * K)], parts)
    parts = lax.all_to_all(send, "dp", 0, 0, axis_index_groups=Y_GROUPS)
    factors, send = call(
        functools.partial(tail_kernel, all_tokens),
        [(K, 2 * K), (NT, 1, EX_DEV * NQ)],
        parts,
        wide,
        scratch=[(K, 2 * K), (4 * SLICE, 2 * K)],
    )
    parts = lax.all_to_all(send, "tensor", 0, 0)
    return tuple(
        call(
            last_kernel,
            [(EX_DEV, K * K), (K, K), (K, K), (EX_DEV, NQ)],
            parts,
            factors,
            wide,
            scratch=[(EX_DEV * QROWS, 2 * K)],
        )
    )


def solution(mesh):
    placed = (
        P("dp", "tensor"),
        P("dp", "tensor"),
        P("tensor", None),
        P("tensor", None),
        P("dp", None),
    )
    return jax.shard_map(
        local,
        mesh=mesh,
        in_specs=placed,
        out_specs=(P("dp", None), P(), P(), P("dp", None)),
        check_vma=False,
    )
```

```python
import functools
import math

import jax
import jax.numpy as jnp
from jax import lax
from jax.experimental import pallas as pl
from jax.experimental.pallas import tpu as pltpu
from jax.sharding import PartitionSpec as P

EX_DEV = 4
TOK_EX = 112
K = 64
NQ = 64
NY = 8
NZ = 8
NT = 8
GRAM = 40
ROWS = 56
QROWS = 32
SLICE = QROWS // NT
UNIT_BLOCKS = (512,) * 7
HI = lax.Precision.HIGHEST
F32 = jnp.float32
VMEM_LIMIT = 16 << 20
WIDE_VMEM_LIMIT = 60 << 20


damping_level = 0.1

Y_GROUPS = [[y * NZ + z for y in range(NY)] for z in range(NZ)]
Z_GROUPS = [[y * NZ + z for z in range(NZ)] for y in range(NY)]


def ldl_inverse(m):
    count = K // 8
    tiles = [m[8 * i : 8 * i + 8] for i in range(count)]
    lane = lax.broadcasted_iota(jnp.int32, (8, 2 * K), 1)
    half = lane & K
    col_of = lane & (K - 1)
    sub = lax.broadcasted_iota(jnp.int32, (8, 2 * K), 0)
    unit, scaled = [], []
    for p in range(count):
        below = range(p, count)
        cols = [
            {t: jnp.take_along_axis(tiles[t], half + (8 * p + s), axis=1) for t in below}
            for s in range(8)
        ]
        inside = (col_of & -8) == 8 * p
        for t in below:
            tiles[t] = jnp.where(inside, 0.0, tiles[t])
        inverses = []
        for s in range(8):
            c = cols[s]
            inv = 1.0 / c[p][s : s + 1]
            inverses.append(inv)
            for j in range(s + 1, 8):
                d = cols[j]
                f = d[p][s : s + 1] * inv
                cols[j] = {t: d[t] - c[t] * f for t in below}
            row = jnp.where(col_of[:1] == 8 * p + s, 1.0, tiles[p][s : s + 1]) * inv
            for t in below:
                new = tiles[t] - c[t] * row
                tiles[t] = jnp.where(sub > s, new, tiles[t]) if t == p else new
        lower = jnp.where(col_of < 8 * p + sub, tiles[p], jnp.where(col_of == 8 * p + sub, 1.0, 0.0))
        unit.append(lower)
        scaled.append(lower * jnp.concatenate(inverses, axis=0))
    both = lax.dot_general(
        jnp.concatenate(unit, axis=0),
        jnp.concatenate(scaled, axis=0),
        (((0,), (0,)), ((), ())),
        precision=HI,
        preferred_element_type=F32,
    )
    return jnp.concatenate([both[:K, :K], both[K:, K:]], axis=1)


def call(body, outs, *args, scratch=(), flops=1 << 20):
    return pl.pallas_call(
        body,
        out_shape=[jax.ShapeDtypeStruct(shape, F32) for shape in outs],
        scratch_shapes=[pltpu.VMEM(shape, F32) for shape in scratch],
        compiler_params=pltpu.CompilerParams(vmem_limit_bytes=VMEM_LIMIT),
        cost_estimate=pl.CostEstimate(flops=flops, bytes_accessed=1 << 20, transcendentals=0),
    )(*args)


def added(ref, rows):
    total = ref[0, rows]
    for i in range(1, ref.shape[0]):
        total = total + ref[i, rows]
    return total


def project_kernel(hidden_ref, grad_ref, win_ref, wout_ref, out_ref, hidden, grad, win, wout, sems):
    contract = (((1,), (1,)), ((), ()))
    wout_copy = pltpu.make_async_copy(wout_ref, wout, sems.at[0])
    grad_copy = pltpu.make_async_copy(grad_ref, grad, sems.at[1])
    win_copy = pltpu.make_async_copy(win_ref, win, sems.at[2])
    wout_copy.start()
    grad_copy.start()
    win_copy.start()
    blocks = []
    first = 0
    for i, size in enumerate(UNIT_BLOCKS):
        units = pl.ds(first, size)
        copy = pltpu.make_async_copy(hidden_ref.at[:, units], hidden.at[:, units], sems.at[3 + i])
        copy.start()
        blocks.append((copy, units))
        first += size
    wout_copy.wait()
    grad_copy.wait()
    out_part = lax.dot_general(wout[...], grad[...], contract, preferred_element_type=F32)
    win_copy.wait()
    in_part = None
    for copy, units in blocks:
        copy.wait()
        part = lax.dot_general(win[:, units], hidden[:, units], contract, preferred_element_type=F32)
        in_part = part if in_part is None else in_part + part
    out_ref[...] = jnp.concatenate([in_part, out_part], axis=0).T.reshape(NT, ROWS, 2 * K)


def project(hidden_act, grad_out, proj_in, proj_out):
    operands = (hidden_act, grad_out, proj_in.T, proj_out.T)
    return pl.pallas_call(
        project_kernel,
        in_specs=[pl.BlockSpec(memory_space=pltpu.HBM)] * len(operands),
        out_shape=jax.ShapeDtypeStruct((NT, ROWS, 2 * K), F32),
        scratch_shapes=[pltpu.VMEM(x.shape, x.dtype) for x in operands]
        + [pltpu.SemaphoreType.DMA((3 + len(UNIT_BLOCKS),))],
        compiler_params=pltpu.CompilerParams(vmem_limit_bytes=WIDE_VMEM_LIMIT),
    )(*operands)


def rows_kernel(parts_ref, send_ref):
    mine = added(parts_ref, pl.ds(0, ROWS))
    for t in range(NT):
        send_ref[t] = mine


def gram_kernel(rows_ref, query_ref, send_ref, wide_ref):
    gram = jnp.zeros((2 * K, 2 * K), F32)
    for e in range(EX_DEV):
        rows = rows_ref[2 * e : 2 * e + 2].reshape(TOK_EX, 2 * K)
        product = lax.dot_general(
            rows, rows, (((0,), (0,)), ((), ())), precision=HI, preferred_element_type=F32
        )
        gram = gram + product
        pair, side = divmod(e, 2)
        grad = product[:K, K:] / math.sqrt(TOK_EX)
        wide_ref[pair * K : (pair + 1) * K, side * K : (side + 1) * K] = grad
    query = query_ref[lax.axis_index("tensor")]
    packed = pack(gram[:K, :K], gram[K:, K:], query)
    for z in range(NZ):
        send_ref[z] = packed


def over_z_kernel(parts_ref, send_ref):
    packed = added(parts_ref, pl.ds(0, GRAM))
    queries = jnp.concatenate([parts_ref[z, GRAM - SLICE :] for z in range(NZ)], axis=0)
    for y in range(NY):
        send_ref[y, :GRAM] = packed
        send_ref[y, GRAM:] = queries


def pack(square_in, square_out, query):
    rows = lax.broadcasted_iota(jnp.int32, (K, K), 0)
    cols = lax.broadcasted_iota(jnp.int32, (K, K), 1)
    square = jnp.where(rows >= cols, square_in, square_out)
    diag = jnp.sum(jnp.where(rows == cols, square_out, 0.0), axis=0, keepdims=True)
    diag = jnp.broadcast_to(jnp.concatenate([diag, diag], axis=1), (SLICE, 2 * K))
    return jnp.concatenate(
        [jnp.concatenate([square[: K // 2], square[K // 2 :]], axis=1), diag, query], axis=0
    )

def unpack(packed):
    rows = lax.broadcasted_iota(jnp.int32, (K, K), 0)
    cols = lax.broadcasted_iota(jnp.int32, (K, K), 1)
    square = jnp.concatenate([packed[: K // 2, :K], packed[: K // 2, K:]], axis=0)
    flipped = square.T
    square_in = jnp.where(rows >= cols, square, flipped)
    square_out = jnp.where(rows < cols, square, flipped)
    square_out = jnp.where(rows == cols, packed[K // 2 : K // 2 + 1, :K], square_out)
    return square_in, square_out

def wide_rows(wide_ref, count):
    blocks = []
    for pair in range(2):
        even = wide_ref[pl.ds(pair * count, count // 2, stride=2), :]
        odd = wide_ref[pl.ds(pair * count + 1, count // 2, stride=2), :]
        blocks.append(jnp.concatenate([even[:, :K], odd[:, :K]], axis=1))
        blocks.append(jnp.concatenate([even[:, K:], odd[:, K:]], axis=1))
    return blocks


def tail_kernel(all_tokens, parts_ref, grads_ref, factors_ref, send_ref, inverse_ref, wide_ref):
    sum_in, sum_out = unpack(added(parts_ref, pl.ds(0, GRAM)))
    rows = lax.broadcasted_iota(jnp.int32, (K, 2 * K), 0)
    cols = lax.broadcasted_iota(jnp.int32, (K, 2 * K), 1)
    eye_mats = jnp.where(rows == (cols & (K - 1)), 1.0, 0.0)
    factors = jnp.concatenate([sum_in, sum_out], axis=1) / all_tokens + damping_level * eye_mats
    factors_ref[...] = factors
    inverse = ldl_inverse(factors)
    inverse_ref[...] = inverse
    count = 2 * SLICE
    mine = inverse_ref[pl.ds(pl.multiple_of(lax.axis_index("tensor") * count, count), count), :]
    out_inv = inverse[:, K:] / float(K)
    zero = jnp.zeros((K, K), F32)
    pair_inv = jnp.concatenate(
        [jnp.concatenate([out_inv, zero], axis=1), jnp.concatenate([zero, out_inv], axis=1)], axis=0
    )
    left = [
        jnp.dot(
            mine[:, :K],
            grads_ref[pair * K : (pair + 1) * K],
            precision=HI,
            preferred_element_type=F32,
        )
        for pair in range(2)
    ]
    wide_ref[...] = jnp.dot(
        jnp.concatenate(left, axis=0), pair_inv, precision=HI, preferred_element_type=F32
    )
    ready = wide_rows(wide_ref, count)
    sums = [[] for _ in range(EX_DEV)]
    for y in range(NY):
        blocks = [parts_ref[y, pl.ds(GRAM + r, NZ, stride=SLICE), :] for r in range(SLICE)]
        for e in range(EX_DEV):
            total = blocks[0] * ready[e][:1]
            for r in range(1, SLICE):
                total = total + blocks[r] * ready[e][r : r + 1]
            sums[e].append(total)
    scores = lax.dot_general(
        jnp.ones((8, 2 * K), F32),
        jnp.concatenate([total for part in sums for total in part], axis=0),
        (((1,), (1,)), ((), ())),
        precision=HI,
        preferred_element_type=F32,
    )
    for t in range(NT):
        send_ref[t] = scores[:1]


def last_kernel(parts_ref, factors_ref, wide_ref, grads_ref, fin_ref, fout_ref, scores_ref, tall_ref):
    total = added(parts_ref, pl.ds(0, 1))
    for e in range(EX_DEV):
        scores_ref[e : e + 1, :] = total[:, e * NQ : (e + 1) * NQ]
    fin_ref[...] = factors_ref[:, :K]
    fout_ref[...] = factors_ref[:, K:]
    for e, block in enumerate(wide_rows(wide_ref, K)):
        tall_ref[e * QROWS : (e + 1) * QROWS] = block
    for r in range(QROWS):
        grads_ref[:, r * 2 * K : (r + 1) * 2 * K] = tall_ref[pl.ds(r, EX_DEV, stride=QROWS), :]


def local(hidden_act, grad_out, proj_in, proj_out, queries):
    all_tokens = float(hidden_act.shape[0] * lax.axis_size("dp"))
    part = project(hidden_act, grad_out, proj_in, proj_out)
    parts = lax.all_to_all(part, "tensor", 0, 0)
    (send,) = call(rows_kernel, [(NT, ROWS, 2 * K)], parts)
    rows = lax.all_to_all(send, "tensor", 0, 0)
    send, wide = call(
        gram_kernel,
        [(NZ, GRAM, 2 * K), (2 * K, 2 * K)],
        rows,
        queries.reshape(NT, SLICE, 2 * K),
    )
    parts = lax.all_to_all(send, "dp", 0, 0, axis_index_groups=Z_GROUPS)
    (send,) = call(over_z_kernel, [(NY, GRAM + QROWS, 2 * K)], parts)
    parts = lax.all_to_all(send, "dp", 0, 0, axis_index_groups=Y_GROUPS)
    factors, send = call(
        functools.partial(tail_kernel, all_tokens),
        [(K, 2 * K), (NT, 1, EX_DEV * NQ)],
        parts,
        wide,
        scratch=[(K, 2 * K), (4 * SLICE, 2 * K)],
    )
    parts = lax.all_to_all(send, "tensor", 0, 0)
    return tuple(
        call(
            last_kernel,
            [(EX_DEV, K * K), (K, K), (K, K), (EX_DEV, NQ)],
            parts,
            factors,
            wide,
            scratch=[(EX_DEV * QROWS, 2 * K)],
        )
    )


def solution(mesh):
    placed = (
        P("dp", "tensor"),
        P("dp", "tensor"),
        P("tensor", None),
        P("tensor", None),
        P("dp", None),
    )
    return jax.shard_map(
        local,
        mesh=mesh,
        in_specs=placed,
        out_specs=(P("dp", None), P(), P(), P("dp", None)),
        check_vma=False,
    )
```

```python
import functools
import math

import jax
import jax.numpy as jnp
from jax import lax
from jax.experimental import pallas as pl
from jax.experimental.pallas import tpu as pltpu
from jax.sharding import PartitionSpec as P

EX_DEV = 4
TOK_EX = 112
K = 64
NQ = 64
NY = 8
NZ = 8
NT = 8
GRAM = 40
ROWS = 56
QROWS = 32
SLICE = QROWS // NT
UNIT_BLOCKS = (1024, 1024, 1024, 512)
HI = lax.Precision.HIGHEST
F32 = jnp.float32
VMEM_LIMIT = 16 << 20
WIDE_VMEM_LIMIT = 60 << 20


damping_level = 0.1

Y_GROUPS = [[y * NZ + z for y in range(NY)] for z in range(NZ)]
Z_GROUPS = [[y * NZ + z for z in range(NZ)] for y in range(NY)]


def ldl_inverse(m):
    count = K // 8
    tiles = [m[8 * i : 8 * i + 8] for i in range(count)]
    lane = lax.broadcasted_iota(jnp.int32, (8, 2 * K), 1)
    half = lane & K
    col_of = lane & (K - 1)
    sub = lax.broadcasted_iota(jnp.int32, (8, 2 * K), 0)
    unit, scaled = [], []
    for p in range(count):
        below = range(p, count)
        cols = [
            {t: jnp.take_along_axis(tiles[t], half + (8 * p + s), axis=1) for t in below}
            for s in range(8)
        ]
        inside = (col_of & -8) == 8 * p
        for t in below:
            tiles[t] = jnp.where(inside, 0.0, tiles[t])
        inverses = []
        for s in range(8):
            c = cols[s]
            inv = 1.0 / c[p][s : s + 1]
            inverses.append(inv)
            for j in range(s + 1, 8):
                d = cols[j]
                f = d[p][s : s + 1] * inv
                cols[j] = {t: d[t] - c[t] * f for t in below}
            row = jnp.where(col_of[:1] == 8 * p + s, 1.0, tiles[p][s : s + 1]) * inv
            for t in below:
                new = tiles[t] - c[t] * row
                tiles[t] = jnp.where(sub > s, new, tiles[t]) if t == p else new
        lower = jnp.where(col_of < 8 * p + sub, tiles[p], jnp.where(col_of == 8 * p + sub, 1.0, 0.0))
        unit.append(lower)
        scaled.append(lower * jnp.concatenate(inverses, axis=0))
    both = lax.dot_general(
        jnp.concatenate(unit, axis=0),
        jnp.concatenate(scaled, axis=0),
        (((0,), (0,)), ((), ())),
        precision=HI,
        preferred_element_type=F32,
    )
    return jnp.concatenate([both[:K, :K], both[K:, K:]], axis=1)


def split(x):
    parts = []
    for _ in range(3):
        parts.append(x.astype(jnp.bfloat16))
        x = x - parts[-1].astype(F32)
    return parts


def call(body, outs, *args, scratch=(), flops=1 << 20):
    return pl.pallas_call(
        body,
        out_shape=[jax.ShapeDtypeStruct(shape, F32) for shape in outs],
        scratch_shapes=[pltpu.VMEM(shape, F32) for shape in scratch],
        compiler_params=pltpu.CompilerParams(vmem_limit_bytes=VMEM_LIMIT),
        cost_estimate=pl.CostEstimate(flops=flops, bytes_accessed=1 << 20, transcendentals=0),
    )(*args)


def added(ref, rows):
    total = ref[0, rows]
    for i in range(1, ref.shape[0]):
        total = total + ref[i, rows]
    return total


def project_kernel(hidden_ref, grad_ref, win_ref, wout_ref, out_ref, hidden, grad, win, wout, sems):
    contract = (((1,), (1,)), ((), ()))
    wout_copy = pltpu.make_async_copy(wout_ref, wout, sems.at[0])
    grad_copy = pltpu.make_async_copy(grad_ref, grad, sems.at[1])
    win_copy = pltpu.make_async_copy(win_ref, win, sems.at[2])
    wout_copy.start()
    grad_copy.start()
    win_copy.start()
    blocks = []
    first = 0
    for i, size in enumerate(UNIT_BLOCKS):
        units = pl.ds(first, size)
        copy = pltpu.make_async_copy(hidden_ref.at[:, units], hidden.at[:, units], sems.at[3 + i])
        copy.start()
        blocks.append((copy, units))
        first += size
    wout_copy.wait()
    grad_copy.wait()
    out_part = lax.dot_general(wout[...], grad[...], contract, preferred_element_type=F32)
    win_copy.wait()
    in_part = None
    for copy, units in blocks:
        copy.wait()
        part = lax.dot_general(win[:, units], hidden[:, units], contract, preferred_element_type=F32)
        in_part = part if in_part is None else in_part + part
    out_ref[...] = jnp.concatenate([in_part, out_part], axis=0).T.reshape(NT, ROWS, 2 * K)


def project(hidden_act, grad_out, proj_in, proj_out):
    operands = (hidden_act, grad_out, proj_in.T, proj_out.T)
    return pl.pallas_call(
        project_kernel,
        in_specs=[pl.BlockSpec(memory_space=pltpu.HBM)] * len(operands),
        out_shape=jax.ShapeDtypeStruct((NT, ROWS, 2 * K), F32),
        scratch_shapes=[pltpu.VMEM(x.shape, x.dtype) for x in operands]
        + [pltpu.SemaphoreType.DMA((3 + len(UNIT_BLOCKS),))],
        compiler_params=pltpu.CompilerParams(vmem_limit_bytes=WIDE_VMEM_LIMIT),
    )(*operands)


def rows_kernel(parts_ref, send_ref):
    mine = added(parts_ref, pl.ds(0, ROWS))
    for t in range(NT):
        send_ref[t] = mine


def gram_kernel(rows_ref, query_ref, send_ref, wide_ref):
    gram = jnp.zeros((2 * K, 2 * K), F32)
    for e in range(EX_DEV):
        rows = rows_ref[2 * e : 2 * e + 2].reshape(TOK_EX, 2 * K)
        product = lax.dot_general(
            rows, rows, (((0,), (0,)), ((), ())), precision=HI, preferred_element_type=F32
        )
        gram = gram + product
        pair, side = divmod(e, 2)
        grad = product[:K, K:] / math.sqrt(TOK_EX)
        wide_ref[pair * K : (pair + 1) * K, side * K : (side + 1) * K] = grad
    query = query_ref[lax.axis_index("tensor")]
    packed = pack(gram[:K, :K], gram[K:, K:], query)
    for z in range(NZ):
        send_ref[z] = packed


def over_z_kernel(parts_ref, send_ref):
    packed = added(parts_ref, pl.ds(0, GRAM))
    queries = jnp.concatenate([parts_ref[z, GRAM - SLICE :] for z in range(NZ)], axis=0)
    for y in range(NY):
        send_ref[y, :GRAM] = packed
        send_ref[y, GRAM:] = queries


def pack(square_in, square_out, query):
    rows = lax.broadcasted_iota(jnp.int32, (K, K), 0)
    cols = lax.broadcasted_iota(jnp.int32, (K, K), 1)
    square = jnp.where(rows >= cols, square_in, square_out)
    diag = jnp.sum(jnp.where(rows == cols, square_out, 0.0), axis=0, keepdims=True)
    diag = jnp.broadcast_to(jnp.concatenate([diag, diag], axis=1), (SLICE, 2 * K))
    return jnp.concatenate(
        [jnp.concatenate([square[: K // 2], square[K // 2 :]], axis=1), diag, query], axis=0
    )

def unpack(packed):
    rows = lax.broadcasted_iota(jnp.int32, (K, K), 0)
    cols = lax.broadcasted_iota(jnp.int32, (K, K), 1)
    square = jnp.concatenate([packed[: K // 2, :K], packed[: K // 2, K:]], axis=0)
    flipped = square.T
    square_in = jnp.where(rows >= cols, square, flipped)
    square_out = jnp.where(rows < cols, square, flipped)
    square_out = jnp.where(rows == cols, packed[K // 2 : K // 2 + 1, :K], square_out)
    return square_in, square_out

def wide_rows(wide_ref, count):
    blocks = []
    for pair in range(2):
        even = wide_ref[pl.ds(pair * count, count // 2, stride=2), :]
        odd = wide_ref[pl.ds(pair * count + 1, count // 2, stride=2), :]
        blocks.append(jnp.concatenate([even[:, :K], odd[:, :K]], axis=1))
        blocks.append(jnp.concatenate([even[:, K:], odd[:, K:]], axis=1))
    return blocks


def tail_kernel(all_tokens, parts_ref, grads_ref, factors_ref, send_ref, inverse_ref, wide_ref):
    sum_in, sum_out = unpack(added(parts_ref, pl.ds(0, GRAM)))
    rows = lax.broadcasted_iota(jnp.int32, (K, 2 * K), 0)
    cols = lax.broadcasted_iota(jnp.int32, (K, 2 * K), 1)
    eye_mats = jnp.where(rows == (cols & (K - 1)), 1.0, 0.0)
    factors = jnp.concatenate([sum_in, sum_out], axis=1) / all_tokens + damping_level * eye_mats
    factors_ref[...] = factors
    inverse = ldl_inverse(factors)
    inverse_ref[...] = inverse
    count = 2 * SLICE
    mine = inverse_ref[pl.ds(pl.multiple_of(lax.axis_index("tensor") * count, count), count), :]
    out_inv = inverse[:, K:] / float(K)
    zero = jnp.zeros((K, K), F32)
    pair_inv = jnp.concatenate(
        [jnp.concatenate([out_inv, zero], axis=1), jnp.concatenate([zero, out_inv], axis=1)], axis=0
    )
    left = [
        jnp.dot(
            mine[:, :K],
            grads_ref[pair * K : (pair + 1) * K],
            precision=HI,
            preferred_element_type=F32,
        )
        for pair in range(2)
    ]
    wide_ref[...] = jnp.dot(
        jnp.concatenate(left, axis=0), pair_inv, precision=HI, preferred_element_type=F32
    )
    ready = wide_rows(wide_ref, count)
    sums = [[] for _ in range(EX_DEV)]
    for y in range(NY):
        blocks = [parts_ref[y, pl.ds(GRAM + r, NZ, stride=SLICE), :] for r in range(SLICE)]
        for e in range(EX_DEV):
            total = blocks[0] * ready[e][:1]
            for r in range(1, SLICE):
                total = total + blocks[r] * ready[e][r : r + 1]
            sums[e].append(total)
    totals = split(jnp.concatenate([total for part in sums for total in part], axis=0))
    ones = jnp.ones((8, 2 * K), jnp.bfloat16)
    scores = [
        lax.dot_general(ones, x, (((1,), (1,)), ((), ())), preferred_element_type=F32)
        for x in totals
    ]
    scores = scores[0] + (scores[1] + scores[2])
    for t in range(NT):
        send_ref[t] = scores[:1]


def last_kernel(parts_ref, factors_ref, wide_ref, grads_ref, fin_ref, fout_ref, scores_ref, tall_ref):
    total = added(parts_ref, pl.ds(0, 1))
    for e in range(EX_DEV):
        scores_ref[e : e + 1, :] = total[:, e * NQ : (e + 1) * NQ]
    fin_ref[...] = factors_ref[:, :K]
    fout_ref[...] = factors_ref[:, K:]
    for e, block in enumerate(wide_rows(wide_ref, K)):
        tall_ref[e * QROWS : (e + 1) * QROWS] = block
    for r in range(QROWS):
        grads_ref[:, r * 2 * K : (r + 1) * 2 * K] = tall_ref[pl.ds(r, EX_DEV, stride=QROWS), :]


def local(hidden_act, grad_out, proj_in, proj_out, queries):
    all_tokens = float(hidden_act.shape[0] * lax.axis_size("dp"))
    part = project(hidden_act, grad_out, proj_in, proj_out)
    parts = lax.all_to_all(part, "tensor", 0, 0)
    (send,) = call(rows_kernel, [(NT, ROWS, 2 * K)], parts)
    rows = lax.all_to_all(send, "tensor", 0, 0)
    send, wide = call(
        gram_kernel,
        [(NZ, GRAM, 2 * K), (2 * K, 2 * K)],
        rows,
        queries.reshape(NT, SLICE, 2 * K),
    )
    parts = lax.all_to_all(send, "dp", 0, 0, axis_index_groups=Z_GROUPS)
    (send,) = call(over_z_kernel, [(NY, GRAM + QROWS, 2 * K)], parts)
    parts = lax.all_to_all(send, "dp", 0, 0, axis_index_groups=Y_GROUPS)
    factors, send = call(
        functools.partial(tail_kernel, all_tokens),
        [(K, 2 * K), (NT, 1, EX_DEV * NQ)],
        parts,
        wide,
        scratch=[(K, 2 * K), (4 * SLICE, 2 * K)],
    )
    parts = lax.all_to_all(send, "tensor", 0, 0)
    return tuple(
        call(
            last_kernel,
            [(EX_DEV, K * K), (K, K), (K, K), (EX_DEV, NQ)],
            parts,
            factors,
            wide,
            scratch=[(EX_DEV * QROWS, 2 * K)],
        )
    )


def solution(mesh):
    placed = (
        P("dp", "tensor"),
        P("dp", "tensor"),
        P("tensor", None),
        P("tensor", None),
        P("dp", None),
    )
    return jax.shard_map(
        local,
        mesh=mesh,
        in_specs=placed,
        out_specs=(P("dp", None), P(), P(), P("dp", None)),
        check_vma=False,
    )
```

```python
import functools
import math

import jax
import jax.numpy as jnp
from jax import lax
from jax.experimental import pallas as pl
from jax.experimental.pallas import tpu as pltpu
from jax.sharding import PartitionSpec as P

EX_DEV = 4
TOK_EX = 112
K = 64
NQ = 64
NY = 8
NZ = 8
NT = 8
GRAM = 40
ROWS = 56
QROWS = 32
SLICE = QROWS // NT
UNIT_BLOCKS = (1024, 1024, 1024, 512)
HI = lax.Precision.HIGHEST
F32 = jnp.float32
VMEM_LIMIT = 16 << 20
WIDE_VMEM_LIMIT = 60 << 20


damping_level = 0.1

Y_GROUPS = [[y * NZ + z for y in range(NY)] for z in range(NZ)]
Z_GROUPS = [[y * NZ + z for z in range(NZ)] for y in range(NY)]


def ldl_inverse(m):
    count = K // 8
    tiles = [m[8 * i : 8 * i + 8] for i in range(count)]
    lane = lax.broadcasted_iota(jnp.int32, (8, 2 * K), 1)
    half = lane & K
    col_of = lane & (K - 1)
    sub = lax.broadcasted_iota(jnp.int32, (8, 2 * K), 0)
    unit, scaled = [], []
    for p in range(count):
        below = range(p, count)
        cols = [
            {t: jnp.take_along_axis(tiles[t], half + (8 * p + s), axis=1) for t in below}
            for s in range(8)
        ]
        inside = (col_of & -8) == 8 * p
        for t in below:
            tiles[t] = jnp.where(inside, 0.0, tiles[t])
        inverses = []
        for s in range(8):
            c = cols[s]
            inv = 1.0 / c[p][s : s + 1]
            inverses.append(inv)
            for j in range(s + 1, 8):
                d = cols[j]
                f = d[p][s : s + 1] * inv
                cols[j] = {t: d[t] - c[t] * f for t in below}
            row = jnp.where(col_of[:1] == 8 * p + s, 1.0, tiles[p][s : s + 1]) * inv
            for t in below:
                new = tiles[t] - c[t] * row
                tiles[t] = jnp.where(sub > s, new, tiles[t]) if t == p else new
        lower = jnp.where(col_of < 8 * p + sub, tiles[p], jnp.where(col_of == 8 * p + sub, 1.0, 0.0))
        unit.append(lower)
        scaled.append(lower * jnp.concatenate(inverses, axis=0))
    both = lax.dot_general(
        jnp.concatenate(unit, axis=0),
        jnp.concatenate(scaled, axis=0),
        (((0,), (0,)), ((), ())),
        precision=HI,
        preferred_element_type=F32,
    )
    return jnp.concatenate([both[:K, :K], both[K:, K:]], axis=1)


def split(x):
    parts = []
    for _ in range(3):
        parts.append(x.astype(jnp.bfloat16))
        x = x - parts[-1].astype(F32)
    return parts


def call(body, outs, *args, scratch=(), flops=1 << 20):
    return pl.pallas_call(
        body,
        out_shape=[jax.ShapeDtypeStruct(shape, F32) for shape in outs],
        scratch_shapes=[pltpu.VMEM(shape, F32) for shape in scratch],
        compiler_params=pltpu.CompilerParams(vmem_limit_bytes=VMEM_LIMIT),
        cost_estimate=pl.CostEstimate(flops=flops, bytes_accessed=1 << 20, transcendentals=0),
    )(*args)


def added(ref, rows):
    total = ref[0, rows]
    for i in range(1, ref.shape[0]):
        total = total + ref[i, rows]
    return total


def project_kernel(hidden_ref, grad_ref, win_ref, wout_ref, out_ref, hidden, grad, win, wout, sems):
    contract = (((1,), (1,)), ((), ()))
    wout_copy = pltpu.make_async_copy(wout_ref, wout, sems.at[0])
    grad_copy = pltpu.make_async_copy(grad_ref, grad, sems.at[1])
    win_copy = pltpu.make_async_copy(win_ref, win, sems.at[2])
    wout_copy.start()
    grad_copy.start()
    win_copy.start()
    blocks = []
    first = 0
    for i, size in enumerate(UNIT_BLOCKS):
        units = pl.ds(first, size)
        copy = pltpu.make_async_copy(hidden_ref.at[:, units], hidden.at[:, units], sems.at[3 + i])
        copy.start()
        blocks.append((copy, units))
        first += size
    wout_copy.wait()
    grad_copy.wait()
    out_part = lax.dot_general(wout[...], grad[...], contract, preferred_element_type=F32)
    win_copy.wait()
    in_part = None
    for copy, units in blocks:
        copy.wait()
        part = lax.dot_general(win[:, units], hidden[:, units], contract, preferred_element_type=F32)
        in_part = part if in_part is None else in_part + part
    out_ref[...] = jnp.concatenate([in_part, out_part], axis=0).T.reshape(NT, ROWS, 2 * K)


def project(hidden_act, grad_out, proj_in, proj_out):
    operands = (hidden_act, grad_out, proj_in.T, proj_out.T)
    return pl.pallas_call(
        project_kernel,
        in_specs=[pl.BlockSpec(memory_space=pltpu.HBM)] * len(operands),
        out_shape=jax.ShapeDtypeStruct((NT, ROWS, 2 * K), F32),
        scratch_shapes=[pltpu.VMEM(x.shape, x.dtype) for x in operands]
        + [pltpu.SemaphoreType.DMA((3 + len(UNIT_BLOCKS),))],
        compiler_params=pltpu.CompilerParams(vmem_limit_bytes=WIDE_VMEM_LIMIT),
    )(*operands)


def rows_kernel(parts_ref, send_ref):
    mine = added(parts_ref, pl.ds(0, ROWS))
    for t in range(NT):
        send_ref[t] = mine


def gram_kernel(rows_ref, query_ref, send_ref, wide_ref):
    gram = jnp.zeros((2 * K, 2 * K), F32)
    for e in range(EX_DEV):
        rows = rows_ref[2 * e : 2 * e + 2].reshape(TOK_EX, 2 * K)
        product = lax.dot_general(
            rows, rows, (((0,), (0,)), ((), ())), precision=HI, preferred_element_type=F32
        )
        gram = gram + product
        pair, side = divmod(e, 2)
        grad = product[:K, K:] / math.sqrt(TOK_EX)
        wide_ref[pair * K : (pair + 1) * K, side * K : (side + 1) * K] = grad
    query = query_ref[lax.axis_index("tensor")]
    packed = pack(gram[:K, :K], gram[K:, K:], query)
    for z in range(NZ):
        send_ref[z] = packed


def over_z_kernel(parts_ref, send_ref):
    packed = added(parts_ref, pl.ds(0, GRAM))
    queries = jnp.concatenate([parts_ref[z, GRAM - SLICE :] for z in range(NZ)], axis=0)
    for y in range(NY):
        send_ref[y, :GRAM] = packed
        send_ref[y, GRAM:] = queries


def pack(square_in, square_out, query):
    rows = lax.broadcasted_iota(jnp.int32, (K, K), 0)
    cols = lax.broadcasted_iota(jnp.int32, (K, K), 1)
    square = jnp.where(rows >= cols, square_in, square_out)
    diag = jnp.sum(jnp.where(rows == cols, square_out, 0.0), axis=0, keepdims=True)
    diag = jnp.broadcast_to(jnp.concatenate([diag, diag], axis=1), (SLICE, 2 * K))
    return jnp.concatenate(
        [jnp.concatenate([square[: K // 2], square[K // 2 :]], axis=1), diag, query], axis=0
    )

def unpack(packed):
    rows = lax.broadcasted_iota(jnp.int32, (K, K), 0)
    cols = lax.broadcasted_iota(jnp.int32, (K, K), 1)
    square = jnp.concatenate([packed[: K // 2, :K], packed[: K // 2, K:]], axis=0)
    flipped = square.T
    square_in = jnp.where(rows >= cols, square, flipped)
    square_out = jnp.where(rows < cols, square, flipped)
    square_out = jnp.where(rows == cols, packed[K // 2 : K // 2 + 1, :K], square_out)
    return square_in, square_out

def wide_rows(wide_ref, count):
    blocks = []
    for pair in range(2):
        even = wide_ref[pl.ds(pair * count, count // 2, stride=2), :]
        odd = wide_ref[pl.ds(pair * count + 1, count // 2, stride=2), :]
        blocks.append(jnp.concatenate([even[:, :K], odd[:, :K]], axis=1))
        blocks.append(jnp.concatenate([even[:, K:], odd[:, K:]], axis=1))
    return blocks


def tail_kernel(all_tokens, parts_ref, grads_ref, factors_ref, send_ref, inverse_ref, wide_ref):
    sum_in, sum_out = unpack(added(parts_ref, pl.ds(0, GRAM)))
    rows = lax.broadcasted_iota(jnp.int32, (K, 2 * K), 0)
    cols = lax.broadcasted_iota(jnp.int32, (K, 2 * K), 1)
    eye_mats = jnp.where(rows == (cols & (K - 1)), 1.0, 0.0)
    factors = jnp.concatenate([sum_in, sum_out], axis=1) / all_tokens + damping_level * eye_mats
    factors_ref[...] = factors
    inverse = ldl_inverse(factors)
    inverse_ref[...] = inverse
    count = 2 * SLICE
    mine = inverse_ref[pl.ds(pl.multiple_of(lax.axis_index("tensor") * count, count), count), :]
    out_inv = inverse[:, K:] / float(K)
    zero = jnp.zeros((K, K), F32)
    pair_inv = jnp.concatenate(
        [jnp.concatenate([out_inv, zero], axis=1), jnp.concatenate([zero, out_inv], axis=1)], axis=0
    )
    grads = jnp.concatenate([grads_ref[:K], grads_ref[K:]], axis=1)
    left = jnp.dot(mine[:, :K], grads, precision=HI, preferred_element_type=F32)
    left = [left[:, : 2 * K], left[:, 2 * K :]]
    wide_ref[...] = jnp.dot(
        jnp.concatenate(left, axis=0), pair_inv, precision=HI, preferred_element_type=F32
    )
    ready = wide_rows(wide_ref, count)
    sums = [[] for _ in range(EX_DEV)]
    for y in range(NY):
        blocks = [parts_ref[y, pl.ds(GRAM + r, NZ, stride=SLICE), :] for r in range(SLICE)]
        for e in range(EX_DEV):
            total = blocks[0] * ready[e][:1]
            for r in range(1, SLICE):
                total = total + blocks[r] * ready[e][r : r + 1]
            sums[e].append(total)
    totals = split(jnp.concatenate([total for part in sums for total in part], axis=0))
    ones = jnp.ones((8, 2 * K), jnp.bfloat16)
    scores = [
        lax.dot_general(ones, x, (((1,), (1,)), ((), ())), preferred_element_type=F32)
        for x in totals
    ]
    scores = scores[0] + (scores[1] + scores[2])
    for t in range(NT):
        send_ref[t] = scores[:1]


def last_kernel(parts_ref, factors_ref, wide_ref, grads_ref, fin_ref, fout_ref, scores_ref, tall_ref):
    total = added(parts_ref, pl.ds(0, 1))
    for e in range(EX_DEV):
        scores_ref[e : e + 1, :] = total[:, e * NQ : (e + 1) * NQ]
    fin_ref[...] = factors_ref[:, :K]
    fout_ref[...] = factors_ref[:, K:]
    for e, block in enumerate(wide_rows(wide_ref, K)):
        tall_ref[e * QROWS : (e + 1) * QROWS] = block
    for r in range(QROWS):
        grads_ref[:, r * 2 * K : (r + 1) * 2 * K] = tall_ref[pl.ds(r, EX_DEV, stride=QROWS), :]


def local(hidden_act, grad_out, proj_in, proj_out, queries):
    all_tokens = float(hidden_act.shape[0] * lax.axis_size("dp"))
    part = project(hidden_act, grad_out, proj_in, proj_out)
    parts = lax.all_to_all(part, "tensor", 0, 0)
    (send,) = call(rows_kernel, [(NT, ROWS, 2 * K)], parts)
    rows = lax.all_to_all(send, "tensor", 0, 0)
    send, wide = call(
        gram_kernel,
        [(NZ, GRAM, 2 * K), (2 * K, 2 * K)],
        rows,
        queries.reshape(NT, SLICE, 2 * K),
    )
    parts = lax.all_to_all(send, "dp", 0, 0, axis_index_groups=Z_GROUPS)
    (send,) = call(over_z_kernel, [(NY, GRAM + QROWS, 2 * K)], parts)
    parts = lax.all_to_all(send, "dp", 0, 0, axis_index_groups=Y_GROUPS)
    factors, send = call(
        functools.partial(tail_kernel, all_tokens),
        [(K, 2 * K), (NT, 1, EX_DEV * NQ)],
        parts,
        wide,
        scratch=[(K, 2 * K), (4 * SLICE, 2 * K)],
    )
    parts = lax.all_to_all(send, "tensor", 0, 0)
    return tuple(
        call(
            last_kernel,
            [(EX_DEV, K * K), (K, K), (K, K), (EX_DEV, NQ)],
            parts,
            factors,
            wide,
            scratch=[(EX_DEV * QROWS, 2 * K)],
        )
    )


def solution(mesh):
    placed = (
        P("dp", "tensor"),
        P("dp", "tensor"),
        P("tensor", None),
        P("tensor", None),
        P("dp", None),
    )
    return jax.shard_map(
        local,
        mesh=mesh,
        in_specs=placed,
        out_specs=(P("dp", None), P(), P(), P("dp", None)),
        check_vma=False,
    )
```
